512 devices in a mesh: grp: 8 (over x, core), vocab: 64 (over y, z).
Axes of the slice: x: 4, y: 4, z: 16, core: 2. Of those that a mesh axis runs over, the one named last changes fastest.
Arguments:
- student_hidden: bfloat16 [1024, 5120], P(('grp', 'vocab')), parts along dimension 0, may hold values from -64 to 64
- teacher_hidden: bfloat16 [1024, 4096], P(('grp', 'vocab')), parts along dimension 0, may hold values from -64 to 64
- student_head: bfloat16 [81920, 5120], P('vocab'), may hold values from -1 to 1
- teacher_head: bfloat16 [81920, 4096], P('vocab'), may hold values from -1 to 1
- row_weight: float32 [1024], P(('grp', 'vocab')), parts along dimension 0, may hold values from 64 to 512
Outputs:
- hidden_grad: bfloat16 [1024, 5120], P(('grp', 'vocab')), parts along dimension 0
The draws below stay inside these ranges and needn't reach their ends.
There are 8 independent parts, one for each index of `grp`. The reference program is written for one: setup_inputs(seed, part) draws one part's arguments, and reference() takes and returns one part's arrays. A program takes and returns all parts, laid end to end along the dimension named above; an argument that names none is the same for every part. Nothing has to cross between parts.
All inputs are finite; a program needn't handle non-finite values.
Results may differ from the reference program's by a relative error of at most 0.0043.
Values may be sent and summed in bfloat16 or wider, within the bound.
No kernel may reach another device: no remote copies, remote signals or barrier semaphores. Data moves between devices by JAX's collectives and lax.ppermute only.
A program may use at most 128 MiB of HBM per device.

```python
import math
import jax
import jax.numpy as jnp
from jax import lax

DS = 5120
DT = 4096
ROWS = 128
VOCAB = 81920


def row_values(key, row_count, width, top_scale):
    keys = jax.random.split(key, 4)
    gaussian = jnp.clip(jax.random.normal(keys[0], (row_count, width), jnp.float32), -3.0, 3.0)
    base_values = gaussian
    row_scale = jnp.exp(jax.random.uniform(keys[2], (row_count, 1), jnp.float32) * jnp.log(top_scale))
    values = base_values * row_scale
    shuffled = jax.random.permutation(keys[3], row_count)
    chosen = shuffled[:3]
    values = values.at[chosen].set(values[chosen])
    return values.astype(jnp.bfloat16)


def head_values(key, entries, width, spread):
    keys = jax.random.split(key, 4)
    gaussian = jnp.clip(jax.random.normal(keys[0], (entries, width), jnp.float32), -4.0, 4.0)
    base_values = gaussian
    row_scale = jnp.exp(jax.random.uniform(keys[2], (entries, 1), jnp.float32, -1.0, 1.0) * jnp.log(spread))
    values = base_values * row_scale / jnp.sqrt(jnp.float32(width))
    first_entry = jax.random.randint(keys[3], (), 0, entries - 1).astype(jnp.int32)
    present = lax.dynamic_slice(values, (first_entry, jnp.int32(0)), (2, width))
    values = lax.dynamic_update_slice(values, present, (first_entry, jnp.int32(0)))
    return values.astype(jnp.bfloat16)


def draw_student_hidden(key, part):
    key = jax.random.fold_in(key, 3)
    return row_values(key, ROWS, DS, 10.0)


def draw_teacher_hidden(key, part):
    key = jax.random.fold_in(key, 5)
    return row_values(key, ROWS, DT, 10.0)


def draw_student_head(key, part):
    key = jax.random.fold_in(key, 7)
    return head_values(key, VOCAB, DS, 2.0)


def draw_teacher_head(key, part):
    key = jax.random.fold_in(key, 11)
    return head_values(key, VOCAB, DT, 2.0)


def block_scale(stream_key, dims, pieces, smallest, largest):
    factor_of, own = 1.0, jax.random.fold_in(stream_key, 6)
    for position, shards_of in pieces:
        heights = jnp.exp(jax.random.uniform(jax.random.fold_in(own, position), (shards_of,), jnp.float32, smallest / len(pieces), largest / len(pieces)))
        factor_of = factor_of * jnp.repeat(heights, dims[position] // shards_of).reshape([-1 if axis == position else 1 for axis in range(len(dims))])
    return factor_of


def setup_inputs(seed: int = 0, part: int = 0) -> dict:
    seeds = jax.random.split(jax.random.key(seed), 6)
    own_keys = jax.random.split(jax.random.fold_in(seeds[5], part), 6)
    return {
        "student_hidden": draw_student_hidden(jax.random.fold_in(jax.random.fold_in(seeds[5], part), 71), part),
        "teacher_hidden": draw_teacher_hidden(jax.random.fold_in(jax.random.fold_in(seeds[5], part), 71), part),
        "student_head": draw_student_head(jax.random.fold_in(seeds[5], 71), part),
        "teacher_head": draw_teacher_head(jax.random.fold_in(seeds[5], 71), part),
        "row_weight": jnp.clip(jnp.exp(math.log(512.0) - 2.0794415 * jax.random.uniform(own_keys[4], (ROWS,), jnp.float32) ** block_scale(own_keys[4], (ROWS,), ((0, 64),), -0.2, 0.2)), 64.0, 512.0),
    }


def probabilities(logits):
    row_top = jnp.max(logits, axis=1, keepdims=True)
    exponent = jnp.exp(logits - row_top)
    return exponent / jnp.sum(exponent, axis=1, keepdims=True)


def reference(student_hidden, teacher_hidden, student_head, teacher_head, row_weight):
    student_logits = jnp.dot(student_hidden, student_head.T, preferred_element_type=jnp.float32)
    teacher_logits = jnp.dot(teacher_hidden, teacher_head.T, preferred_element_type=jnp.float32)
    difference = (probabilities(student_logits) - probabilities(teacher_logits)).astype(jnp.bfloat16)
    summed = jnp.dot(difference, student_head, preferred_element_type=jnp.float32)
    return (row_weight[:, None] * summed).astype(jnp.bfloat16)
```

```python
import jax
import jax.numpy as jnp
from jax import lax
from jax.sharding import Mesh, PartitionSpec as P

Y, Z = 4, 16
DIMS = (((1,), (1,)), ((), ()))


def to_all(x, axis, size):
    return lax.all_to_all(jnp.broadcast_to(x[None], (size, *x.shape)), axis, 0, 0)


def local(student_hidden, teacher_hidden, student_head, teacher_head, row_weight):
    ds, dt = student_hidden.shape[1], teacher_hidden.shape[1]
    mine = jnp.concatenate([student_hidden, teacher_hidden], axis=1)
    plane = to_all(mine, "z", Z).reshape(Z * 2, ds + dt)
    student_rows = to_all(plane[:, :ds], "y", Y).reshape(Y * Z * 2, ds)
    teacher_rows = to_all(plane[:, ds:], "y", Y).reshape(Y * Z * 2, dt)
    student_logits = lax.dot_general(student_rows, student_head, DIMS, preferred_element_type=jnp.float32)
    teacher_logits = lax.dot_general(teacher_rows, teacher_head, DIMS, preferred_element_type=jnp.float32)
    student_top = jnp.max(student_logits, axis=1)
    teacher_top = jnp.max(teacher_logits, axis=1)
    student_exp = jnp.exp(student_logits - student_top[:, None])
    teacher_exp = jnp.exp(teacher_logits - teacher_top[:, None])
    stats = jnp.stack(
        [student_top, teacher_top, jnp.sum(student_exp, axis=1), jnp.sum(teacher_exp, axis=1)]
    )
    every = to_all(stats, ("y", "z"), Y * Z)
    tops = jnp.max(every[:, :2], axis=0)
    totals = jnp.sum(every[:, 2:] * jnp.exp(every[:, :2] - tops), axis=0)
    factors = jnp.exp(stats[:2] - tops) / totals
    difference = (student_exp * factors[0][:, None] - teacher_exp * factors[1][:, None]).astype(jnp.bfloat16)
    partial = jnp.dot(difference, student_head, preferred_element_type=jnp.float32).astype(jnp.bfloat16)
    over_y = lax.all_to_all(partial.reshape(Y, Z * 2, ds), "y", 0, 0)
    over_y = jnp.sum(over_y.astype(jnp.float32), axis=0).astype(jnp.bfloat16)
    over_z = lax.all_to_all(over_y.reshape(Z, 2, ds), "z", 0, 0)
    summed = jnp.sum(over_z.astype(jnp.float32), axis=0)
    return (row_weight[:, None] * summed).astype(jnp.bfloat16)


def solution(mesh):
    split = Mesh(mesh.devices.reshape(-1, Y, Z), ("grp", "y", "z"))
    rows = P(("grp", "y", "z"))
    head = P(("y", "z"))
    return jax.shard_map(
        local, mesh=split, in_specs=(rows, rows, head, head, rows), out_specs=rows, check_vma=False
    )
```

```python
import jax
import jax.numpy as jnp
from jax import lax
from jax.experimental import pallas as pl
from jax.experimental.pallas import tpu as pltpu
from jax.sharding import Mesh, PartitionSpec as P

Y, Z, L = 4, 16, 2
H = Z // L
NEAR, FAR, ALL = ("y", "l"), "h", ("y", "h", "l")
DIMS = (((1,), (1,)), ((), ()))
MIB = 1 << 20
WIDE, DEEP = 512, 256
IN_VMEM = pl.BlockSpec(memory_space=pltpu.VMEM)
IN_HBM = pl.BlockSpec(memory_space=pltpu.HBM)


def to_all(x, axis, size):
    return lax.all_to_all(jnp.broadcast_to(x[None], (size, *x.shape)), axis, 0, 0)


def far_off(x):
    return pltpu.with_memory_space_constraint(x, pltpu.HBM)


def near(x):
    return pltpu.with_memory_space_constraint(x, pltpu.VMEM)


def spread_kernel(far_ref, out_ref):
    far = far_ref[...].astype(jnp.float32)
    block = jnp.concatenate([far[i] for i in range(far.shape[0])], axis=0).astype(out_ref.dtype)
    for i in range(out_ref.shape[0]):
        out_ref[i] = block


def spread(far):
    count, rows, width = far.shape
    return pl.pallas_call(
        spread_kernel,
        out_shape=jax.ShapeDtypeStruct((Y * L, count * rows, width), far.dtype),
        in_specs=[IN_VMEM],
        out_specs=IN_VMEM,
        compiler_params=pltpu.CompilerParams(vmem_limit_bytes=8 * MIB),
    )(far)


def fold_kernel(sums_ref, out_ref):
    total = jnp.sum(sums_ref[...].astype(jnp.float32), axis=0)
    for i in range(out_ref.shape[0]):
        out_ref[i] = total[2 * i : 2 * i + 2].astype(out_ref.dtype)


def fold(sums):
    width = sums.shape[2]
    return pl.pallas_call(
        fold_kernel,
        out_shape=jax.ShapeDtypeStruct((H, 2, width), sums.dtype),
        in_specs=[IN_VMEM],
        out_specs=IN_VMEM,
        compiler_params=pltpu.CompilerParams(vmem_limit_bytes=8 * MIB),
    )(sums)


def logits_kernel(
    rows_ref, student_far, teacher_far, student_exp, teacher_exp, stats_ref, student_near, teacher_near, sems
):
    rows = rows_ref.shape[0]
    pieces = student_far.shape[0] // DEEP
    heads = ((student_far, student_near, student_exp), (teacher_far, teacher_near, teacher_exp))

    def copy(k, i):
        part = pl.ds(i * DEEP, DEEP)
        return pltpu.make_async_copy(heads[k][0].at[part], heads[k][1].at[part], sems.at[k, i])

    for k in range(2):
        for i in range(pieces):
            copy(k, i).start()
    lane = lax.broadcasted_iota(jnp.int32, (rows, rows), 1)
    stats = jnp.zeros((rows, rows), jnp.float32)
    first = 0
    for k, (_, head, out) in enumerate(heads):
        width = head.shape[1]
        top = None
        for i in range(pieces):
            copy(k, i).wait()
            part = slice(i * DEEP, (i + 1) * DEEP)
            piece = lax.dot_general(
                rows_ref[:, first : first + width], head[part, :], DIMS, preferred_element_type=jnp.float32
            )
            out[:, part] = piece
            most = jnp.max(piece, axis=1, keepdims=True)
            top = most if top is None else jnp.maximum(top, most)
        exp = jnp.exp(out[...] - top)
        out[...] = exp
        total = jnp.sum(exp, axis=1, keepdims=True)
        stats = jnp.where(lane == k, top, jnp.where(lane == 2 + k, total, stats))
        first += width
    stats_ref[...] = jnp.transpose(stats)[:4]


def logits(every, student_head, teacher_head):
    rows, entries = every.shape[0], student_head.shape[0]
    return pl.pallas_call(
        logits_kernel,
        out_shape=(
            jax.ShapeDtypeStruct((rows, entries), jnp.float32),
            jax.ShapeDtypeStruct((rows, entries), jnp.float32),
            jax.ShapeDtypeStruct((4, rows), jnp.float32),
            pltpu.VMEM(student_head.shape, student_head.dtype),
        ),
        in_specs=[IN_VMEM, IN_HBM, IN_HBM],
        out_specs=[IN_VMEM] * 4,
        scratch_shapes=[
            pltpu.VMEM(teacher_head.shape, teacher_head.dtype),
            pltpu.SemaphoreType.DMA((2, entries // DEEP)),
        ],
        compiler_params=pltpu.CompilerParams(vmem_limit_bytes=24 * MIB),
    )(every, far_off(student_head), far_off(teacher_head))


def partial_kernel(student_exp, teacher_exp, stats_ref, all_ref, head, out, difference):
    rows = student_exp.shape[0]
    tops = jnp.max(all_ref[:, :2], axis=0)
    totals = jnp.sum(all_ref[:, 2:] * jnp.exp(all_ref[:, :2] - tops), axis=0)
    factors = jnp.exp(stats_ref[:2] - tops) / totals
    student_factor = jnp.transpose(jnp.broadcast_to(factors[0:1], (rows, rows)))
    teacher_factor = jnp.transpose(jnp.broadcast_to(factors[1:2], (rows, rows)))
    for i in range(student_exp.shape[1] // rows):
        part = slice(i * rows, (i + 1) * rows)
        difference[:, part] = (
            student_exp[:, part] * student_factor - teacher_exp[:, part] * teacher_factor
        ).astype(difference.dtype)

    @pl.loop(0, out.shape[1] // WIDE)
    def _(i):
        part = pl.ds(pl.multiple_of(i * WIDE, WIDE), WIDE)
        out[:, part] = jnp.dot(
            difference[...], head[:, part], preferred_element_type=jnp.float32
        ).astype(out.dtype)


def partial(student_exp, teacher_exp, stats, stats_of, head):
    rows, entries = student_exp.shape
    return pl.pallas_call(
        partial_kernel,
        out_shape=jax.ShapeDtypeStruct((rows, head.shape[1]), jnp.bfloat16),
        in_specs=[IN_VMEM] * 5,
        out_specs=IN_VMEM,
        scratch_shapes=[pltpu.VMEM((rows, entries), jnp.bfloat16)],
        compiler_params=pltpu.CompilerParams(vmem_limit_bytes=12 * MIB),
    )(student_exp, teacher_exp, stats, stats_of, near(head))


def local(student_hidden, teacher_hidden, student_head, teacher_head, row_weight):
    ds, dt = student_hidden.shape[1], teacher_hidden.shape[1]
    mine = jnp.concatenate([student_hidden, teacher_hidden], axis=1)
    far = to_all(mine, FAR, H)
    every = lax.all_to_all(spread(far), NEAR, 0, 0).reshape(Y * Z * 2, ds + dt)
    student_exp, teacher_exp, stats, student_near = logits(every, student_head, teacher_head)
    stats_of = to_all(stats, ALL, Y * Z)
    sums = partial(student_exp, teacher_exp, stats, stats_of, student_near)
    near_sums = lax.all_to_all(sums.reshape(Y * L, H * 2, ds), NEAR, 0, 0)
    far_sums = lax.all_to_all(fold(near_sums), FAR, 0, 0)
    summed = jnp.sum(far_sums.astype(jnp.float32), axis=0)
    return (row_weight[:, None] * summed).astype(jnp.bfloat16)


def solution(mesh):
    split = Mesh(mesh.devices.reshape(-1, Y, H, L), ("grp", "y", "h", "l"))
    rows = P(("grp", *ALL))
    head = P(ALL)
    return jax.shard_map(
        local, mesh=split, in_specs=(rows, rows, head, head, rows), out_specs=rows, check_vma=False
    )
```

```python
import jax
import jax.numpy as jnp
from jax import lax
from jax.experimental import pallas as pl
from jax.experimental.pallas import tpu as pltpu
from jax.sharding import Mesh, PartitionSpec as P

Y, Z, L = 4, 16, 2
H = Z // L
NEAR, FAR, ALL = ("y", "l"), "h", ("y", "h", "l")
DIMS = (((1,), (1,)), ((), ()))
MIB = 1 << 20
WIDE, DEEP = 512, 640
IN_VMEM = pl.BlockSpec(memory_space=pltpu.VMEM)
IN_HBM = pl.BlockSpec(memory_space=pltpu.HBM)


def to_all(x, axis, size):
    return lax.all_to_all(jnp.broadcast_to(x[None], (size, *x.shape)), axis, 0, 0)


def far_off(x):
    return pltpu.with_memory_space_constraint(x, pltpu.HBM)


def near(x):
    return pltpu.with_memory_space_constraint(x, pltpu.VMEM)


def spread_kernel(far_ref, student_head, teacher_head, out_ref):
    far = far_ref[...].astype(jnp.float32)
    block = jnp.concatenate([far[i] for i in range(far.shape[0])], axis=0).astype(out_ref.dtype)
    for i in range(out_ref.shape[0]):
        out_ref[i] = block


def spread(far, student_head, teacher_head):
    count, rows, width = far.shape
    return pl.pallas_call(
        spread_kernel,
        out_shape=jax.ShapeDtypeStruct((Y * L, count * rows, width), far.dtype),
        in_specs=[IN_VMEM, IN_HBM, IN_HBM],
        out_specs=IN_VMEM,
        compiler_params=pltpu.CompilerParams(vmem_limit_bytes=8 * MIB),
    )(far, far_off(student_head), far_off(teacher_head))


def fold_kernel(sums_ref, out_ref):
    total = jnp.sum(sums_ref[...].astype(jnp.float32), axis=0)
    for i in range(out_ref.shape[0]):
        out_ref[i] = total[2 * i : 2 * i + 2].astype(out_ref.dtype)


def fold(sums):
    width = sums.shape[2]
    return pl.pallas_call(
        fold_kernel,
        out_shape=jax.ShapeDtypeStruct((H, 2, width), sums.dtype),
        in_specs=[IN_VMEM],
        out_specs=IN_VMEM,
        compiler_params=pltpu.CompilerParams(vmem_limit_bytes=8 * MIB),
    )(sums)


def logits_kernel(rows_ref, student_ref, teacher_ref, student_exp, teacher_exp, stats_ref, scratch):
    rows = rows_ref.shape[0]
    first = 0
    for k, (head, out) in enumerate(((student_ref, student_exp), (teacher_ref, teacher_exp))):
        entries, width = head.shape
        top = None
        for i in range(entries // DEEP):
            part = slice(i * DEEP, (i + 1) * DEEP)
            piece = lax.dot_general(
                head[part, :], rows_ref[:, first : first + width], DIMS, preferred_element_type=jnp.float32
            )
            scratch[part, :] = piece
            most = jnp.max(piece, axis=0, keepdims=True)
            top = most if top is None else jnp.maximum(top, most)
        total = jnp.zeros_like(top)
        for i in range(entries // rows):
            part = slice(i * rows, (i + 1) * rows)
            exp = jnp.exp(scratch[part, :] - top)
            total += jnp.sum(exp, axis=0, keepdims=True)
            out[:, part] = jnp.transpose(exp)
        stats_ref[k : k + 1] = top
        stats_ref[2 + k : 3 + k] = total
        first += width


def logits(every, student_head, teacher_head):
    rows, entries = every.shape[0], student_head.shape[0]
    return pl.pallas_call(
        logits_kernel,
        out_shape=(
            jax.ShapeDtypeStruct((rows, entries), jnp.float32),
            jax.ShapeDtypeStruct((rows, entries), jnp.float32),
            jax.ShapeDtypeStruct((4, rows), jnp.float32),
        ),
        in_specs=[IN_VMEM] * 3,
        out_specs=[IN_VMEM] * 3,
        scratch_shapes=[pltpu.VMEM((entries, rows), jnp.float32)],
        compiler_params=pltpu.CompilerParams(vmem_limit_bytes=12 * MIB),
    )(every, near(student_head), near(teacher_head))


def partial_kernel(student_exp, teacher_exp, stats_ref, all_ref, head, out, difference):
    rows = student_exp.shape[0]
    tops = jnp.max(all_ref[:, :2], axis=0)
    totals = jnp.sum(all_ref[:, 2:] * jnp.exp(all_ref[:, :2] - tops), axis=0)
    factors = jnp.exp(stats_ref[:2] - tops) / totals
    student_factor = jnp.transpose(jnp.broadcast_to(factors[0:1], (rows, rows)))
    teacher_factor = jnp.transpose(jnp.broadcast_to(factors[1:2], (rows, rows)))
    for i in range(student_exp.shape[1] // rows):
        part = slice(i * rows, (i + 1) * rows)
        difference[:, part] = (
            student_exp[:, part] * student_factor - teacher_exp[:, part] * teacher_factor
        ).astype(difference.dtype)

    @pl.loop(0, out.shape[1] // WIDE)
    def _(i):
        part = pl.ds(pl.multiple_of(i * WIDE, WIDE), WIDE)
        out[:, part] = jnp.dot(
            difference[...], head[:, part], preferred_element_type=jnp.float32
        ).astype(out.dtype)


def partial(student_exp, teacher_exp, stats, stats_of, head):
    rows, entries = student_exp.shape
    return pl.pallas_call(
        partial_kernel,
        out_shape=jax.ShapeDtypeStruct((rows, head.shape[1]), jnp.bfloat16),
        in_specs=[IN_VMEM] * 5,
        out_specs=IN_VMEM,
        scratch_shapes=[pltpu.VMEM((rows, entries), jnp.bfloat16)],
        compiler_params=pltpu.CompilerParams(vmem_limit_bytes=12 * MIB),
    )(student_exp, teacher_exp, stats, stats_of, near(head))


def local(student_hidden, teacher_hidden, student_head, teacher_head, row_weight):
    ds, dt = student_hidden.shape[1], teacher_hidden.shape[1]
    mine = jnp.concatenate([student_hidden, teacher_hidden], axis=1)
    far = to_all(mine, FAR, H)
    every = lax.all_to_all(spread(far, student_head, teacher_head), NEAR, 0, 0).reshape(Y * Z * 2, ds + dt)
    student_exp, teacher_exp, stats = logits(every, student_head, teacher_head)
    stats_of = to_all(stats, ALL, Y * Z)
    sums = partial(student_exp, teacher_exp, stats, stats_of, student_head)
    near_sums = lax.all_to_all(sums.reshape(Y * L, H * 2, ds), NEAR, 0, 0)
    far_sums = lax.all_to_all(fold(near_sums), FAR, 0, 0)
    summed = jnp.sum(far_sums.astype(jnp.float32), axis=0)
    return (row_weight[:, None] * summed).astype(jnp.bfloat16)


def solution(mesh):
    split = Mesh(mesh.devices.reshape(-1, Y, H, L), ("grp", "y", "h", "l"))
    rows = P(("grp", *ALL))
    head = P(ALL)
    return jax.shard_map(
        local, mesh=split, in_specs=(rows, rows, head, head, rows), out_specs=rows, check_vma=False
    )
```

```python
import jax
import jax.numpy as jnp
from jax import lax
from jax.experimental import pallas as pl
from jax.experimental.pallas import tpu as pltpu
from jax.sharding import Mesh, PartitionSpec as P

Y, Z, L = 4, 16, 2
H = Z // L
NEAR, FAR, ALL = ("y", "l"), "h", ("y", "h", "l")
DIMS = (((1,), (1,)), ((), ()))
MIB = 1 << 20
WIDE, DEEP = 2560, 256
IN_VMEM = pl.BlockSpec(memory_space=pltpu.VMEM)
IN_HBM = pl.BlockSpec(memory_space=pltpu.HBM)


def to_all(x, axis, size):
    return lax.all_to_all(jnp.broadcast_to(x[None], (size, *x.shape)), axis, 0, 0)


def far_off(x):
    return pltpu.with_memory_space_constraint(x, pltpu.HBM)


def near(x):
    return pltpu.with_memory_space_constraint(x, pltpu.VMEM)


def spread_kernel(far_ref, student_head, teacher_head, out_ref):
    far = far_ref[...].astype(jnp.float32)
    block = jnp.concatenate([far[i] for i in range(far.shape[0])], axis=0).astype(out_ref.dtype)
    for i in range(out_ref.shape[0]):
        out_ref[i] = block


def spread(far, student_head, teacher_head):
    count, rows, width = far.shape
    return pl.pallas_call(
        spread_kernel,
        out_shape=jax.ShapeDtypeStruct((Y * L, count * rows, width), far.dtype),
        in_specs=[IN_VMEM, IN_HBM, IN_HBM],
        out_specs=IN_VMEM,
        compiler_params=pltpu.CompilerParams(vmem_limit_bytes=8 * MIB),
    )(far, far_off(student_head), far_off(teacher_head))


def fold_kernel(sums_ref, out_ref):
    total = jnp.sum(sums_ref[...].astype(jnp.float32), axis=0)
    for i in range(out_ref.shape[0]):
        out_ref[i] = total[2 * i : 2 * i + 2].astype(out_ref.dtype)


def fold(sums):
    width = sums.shape[2]
    return pl.pallas_call(
        fold_kernel,
        out_shape=jax.ShapeDtypeStruct((H, 2, width), sums.dtype),
        in_specs=[IN_VMEM],
        out_specs=IN_VMEM,
        compiler_params=pltpu.CompilerParams(vmem_limit_bytes=8 * MIB),
    )(sums)


def finish_kernel(sums_ref, weight_ref, out_ref):
    summed = jnp.sum(sums_ref[...].astype(jnp.float32), axis=0)
    row = lax.broadcasted_iota(jnp.int32, summed.shape, 0)
    out_ref[...] = (jnp.where(row == 0, weight_ref[0], weight_ref[1]) * summed).astype(out_ref.dtype)


def finish(sums, row_weight):
    return pl.pallas_call(
        finish_kernel,
        out_shape=jax.ShapeDtypeStruct(sums.shape[1:], sums.dtype),
        in_specs=[IN_VMEM, pl.BlockSpec(memory_space=pltpu.SMEM)],
        out_specs=IN_VMEM,
        compiler_params=pltpu.CompilerParams(vmem_limit_bytes=4 * MIB),
    )(sums, row_weight)


def logits_kernel(rows_ref, student_ref, teacher_ref, student_exp, teacher_exp, tops_ref, sums_ref, scratch):
    rows = rows_ref.shape[0]
    first = 0
    for k, (head, out) in enumerate(((student_ref, student_exp), (teacher_ref, teacher_exp))):
        entries, width = head.shape
        top = None
        for i in range(entries // DEEP):
            part = slice(i * DEEP, (i + 1) * DEEP)
            piece = lax.dot_general(
                head[part, :], rows_ref[:, first : first + width], DIMS, preferred_element_type=jnp.float32
            )
            scratch[part, :] = piece
            most = jnp.max(piece, axis=0, keepdims=True)
            top = most if top is None else jnp.maximum(top, most)
        total = jnp.zeros_like(top)
        for i in range(entries // rows):
            part = slice(i * rows, (i + 1) * rows)
            exp = jnp.exp(scratch[part, :] - top)
            total += jnp.sum(exp, axis=0, keepdims=True)
            out[:, part] = jnp.transpose(exp)
        tops_ref[k : k + 1] = top
        sums_ref[k : k + 1] = top + jnp.log(total)
        first += width


def logits(every, student_head, teacher_head):
    rows, entries = every.shape[0], student_head.shape[0]
    return pl.pallas_call(
        logits_kernel,
        out_shape=(
            jax.ShapeDtypeStruct((rows, entries), jnp.float32),
            jax.ShapeDtypeStruct((rows, entries), jnp.float32),
            jax.ShapeDtypeStruct((2, rows), jnp.float32),
            jax.ShapeDtypeStruct((2, rows), jnp.float32),
        ),
        in_specs=[IN_VMEM] * 3,
        out_specs=[IN_VMEM] * 4,
        scratch_shapes=[pltpu.VMEM((entries, rows), jnp.float32)],
        compiler_params=pltpu.CompilerParams(vmem_limit_bytes=12 * MIB),
    )(every, near(student_head), near(teacher_head))


def partial_kernel(student_exp, teacher_exp, tops_ref, all_ref, head, out, difference):
    rows = student_exp.shape[0]
    most = jnp.max(all_ref[...], axis=0)
    total = jnp.sum(jnp.exp(all_ref[...] - most), axis=0)
    factors = jnp.exp(tops_ref[...] - most) / total
    student_factor = jnp.transpose(jnp.broadcast_to(factors[0:1], (rows, rows)))
    teacher_factor = jnp.transpose(jnp.broadcast_to(factors[1:2], (rows, rows)))
    for i in range(student_exp.shape[1] // rows):
        part = slice(i * rows, (i + 1) * rows)
        difference[:, part] = (
            student_exp[:, part] * student_factor - teacher_exp[:, part] * teacher_factor
        ).astype(difference.dtype)

    for i in range(out.shape[1] // WIDE):
        part = slice(i * WIDE, (i + 1) * WIDE)
        out[:, part] = jnp.dot(
            difference[...], head[:, part], preferred_element_type=jnp.float32
        ).astype(out.dtype)


def partial(student_exp, teacher_exp, tops, sums_of, head):
    rows, entries = student_exp.shape
    return pl.pallas_call(
        partial_kernel,
        out_shape=jax.ShapeDtypeStruct((rows, head.shape[1]), jnp.bfloat16),
        in_specs=[IN_VMEM] * 5,
        out_specs=IN_VMEM,
        scratch_shapes=[pltpu.VMEM((rows, entries), jnp.bfloat16)],
        compiler_params=pltpu.CompilerParams(vmem_limit_bytes=12 * MIB),
    )(student_exp, teacher_exp, tops, sums_of, near(head))


def local(student_hidden, teacher_hidden, student_head, teacher_head, row_weight):
    ds, dt = student_hidden.shape[1], teacher_hidden.shape[1]
    mine = jnp.concatenate([student_hidden, teacher_hidden], axis=1)
    far = to_all(mine, FAR, H)
    every = lax.all_to_all(spread(far, student_head, teacher_head), NEAR, 0, 0).reshape(Y * Z * 2, ds + dt)
    student_exp, teacher_exp, tops, log_sums = logits(every, student_head, teacher_head)
    log_sums_of = to_all(log_sums, ALL, Y * Z)
    parts = partial(student_exp, teacher_exp, tops, log_sums_of, student_head)
    near_sums = lax.all_to_all(parts.reshape(Y * L, H * 2, ds), NEAR, 0, 0)
    far_sums = lax.all_to_all(fold(near_sums), FAR, 0, 0)
    return finish(far_sums, row_weight)


def solution(mesh):
    split = Mesh(mesh.devices.reshape(-1, Y, H, L), ("grp", "y", "h", "l"))
    rows = P(("grp", *ALL))
    head = P(ALL)
    return jax.shard_map(
        local, mesh=split, in_specs=(rows, rows, head, head, rows), out_specs=rows, check_vma=False
    )
```

```python
import jax
import jax.numpy as jnp
from jax import lax
from jax.experimental import pallas as pl
from jax.experimental.pallas import tpu as pltpu
from jax.sharding import Mesh, PartitionSpec as P

Y, Z, L = 4, 16, 2
H = Z // L
NEAR, FAR, ALL = ("y", "l"), "h", ("y", "h", "l")
DIMS = (((1,), (1,)), ((), ()))
MIB = 1 << 20
WIDE, DEEP = 2560, 256
IN_VMEM = pl.BlockSpec(memory_space=pltpu.VMEM)
IN_HBM = pl.BlockSpec(memory_space=pltpu.HBM)


def to_all(x, axis, size):
    return lax.all_to_all(jnp.broadcast_to(x[None], (size, *x.shape)), axis, 0, 0)


def far_off(x):
    return pltpu.with_memory_space_constraint(x, pltpu.HBM)


def near(x):
    return pltpu.with_memory_space_constraint(x, pltpu.VMEM)


def spread_kernel(far_ref, student_head, teacher_head, out_ref):
    far = far_ref[...].astype(jnp.float32)
    block = jnp.concatenate([far[i] for i in range(far.shape[0])], axis=0).astype(out_ref.dtype)
    for i in range(out_ref.shape[0]):
        out_ref[i] = block


def spread(far, student_head, teacher_head):
    count, rows, width = far.shape
    return pl.pallas_call(
        spread_kernel,
        out_shape=jax.ShapeDtypeStruct((Y * L, count * rows, width), far.dtype),
        in_specs=[IN_VMEM, IN_HBM, IN_HBM],
        out_specs=IN_VMEM,
        compiler_params=pltpu.CompilerParams(vmem_limit_bytes=8 * MIB),
    )(far, far_off(student_head), far_off(teacher_head))


def fold_kernel(sums_ref, out_ref):
    total = jnp.sum(sums_ref[...].astype(jnp.float32), axis=0)
    for i in range(out_ref.shape[0]):
        out_ref[i] = total[2 * i : 2 * i + 2].astype(out_ref.dtype)


def fold(sums):
    width = sums.shape[2]
    return pl.pallas_call(
        fold_kernel,
        out_shape=jax.ShapeDtypeStruct((H, 2, width), sums.dtype),
        in_specs=[IN_VMEM],
        out_specs=IN_VMEM,
        compiler_params=pltpu.CompilerParams(vmem_limit_bytes=8 * MIB),
    )(sums)


def logits_kernel(rows_ref, student_ref, teacher_ref, student_exp, teacher_exp, tops_ref, sums_ref, scratch):
    rows = rows_ref.shape[0]
    first = 0
    for k, (head, out) in enumerate(((student_ref, student_exp), (teacher_ref, teacher_exp))):
        entries, width = head.shape
        top = None
        for i in range(entries // DEEP):
            part = slice(i * DEEP, (i + 1) * DEEP)
            piece = lax.dot_general(
                head[part, :], rows_ref[:, first : first + width], DIMS, preferred_element_type=jnp.float32
            )
            scratch[part, :] = piece
            most = jnp.max(piece, axis=0, keepdims=True)
            top = most if top is None else jnp.maximum(top, most)
        total = jnp.zeros_like(top)
        for i in range(entries // rows):
            part = slice(i * rows, (i + 1) * rows)
            exp = jnp.exp(scratch[part, :] - top)
            total += jnp.sum(exp, axis=0, keepdims=True)
            out[:, part] = jnp.transpose(exp)
        tops_ref[k : k + 1] = top
        sums_ref[k : k + 1] = top + jnp.log(total)
        first += width


def logits(every, student_head, teacher_head):
    rows, entries = every.shape[0], student_head.shape[0]
    return pl.pallas_call(
        logits_kernel,
        out_shape=(
            jax.ShapeDtypeStruct((rows, entries), jnp.float32),
            jax.ShapeDtypeStruct((rows, entries), jnp.float32),
            jax.ShapeDtypeStruct((2, rows), jnp.float32),
            jax.ShapeDtypeStruct((2, rows), jnp.float32),
        ),
        in_specs=[IN_VMEM] * 3,
        out_specs=[IN_VMEM] * 4,
        scratch_shapes=[pltpu.VMEM((entries, rows), jnp.float32)],
        compiler_params=pltpu.CompilerParams(vmem_limit_bytes=12 * MIB),
    )(every, near(student_head), near(teacher_head))


def partial_kernel(student_exp, teacher_exp, tops_ref, all_ref, head, out, difference):
    rows = student_exp.shape[0]
    most = jnp.max(all_ref[...], axis=0)
    total = jnp.sum(jnp.exp(all_ref[...] - most), axis=0)
    factors = jnp.exp(tops_ref[...] - most) / total
    student_factor = jnp.transpose(jnp.broadcast_to(factors[0:1], (rows, rows)))
    teacher_factor = jnp.transpose(jnp.broadcast_to(factors[1:2], (rows, rows)))
    for i in range(student_exp.shape[1] // rows):
        part = slice(i * rows, (i + 1) * rows)
        difference[:, part] = (
            student_exp[:, part] * student_factor - teacher_exp[:, part] * teacher_factor
        ).astype(difference.dtype)

    for i in range(out.shape[1] // WIDE):
        part = slice(i * WIDE, (i + 1) * WIDE)
        out[:, part] = jnp.dot(
            difference[...], head[:, part], preferred_element_type=jnp.float32
        ).astype(out.dtype)


def partial(student_exp, teacher_exp, tops, sums_of, head):
    rows, entries = student_exp.shape
    return pl.pallas_call(
        partial_kernel,
        out_shape=jax.ShapeDtypeStruct((rows, head.shape[1]), jnp.bfloat16),
        in_specs=[IN_VMEM] * 5,
        out_specs=IN_VMEM,
        scratch_shapes=[pltpu.VMEM((rows, entries), jnp.bfloat16)],
        compiler_params=pltpu.CompilerParams(vmem_limit_bytes=12 * MIB),
    )(student_exp, teacher_exp, tops, sums_of, near(head))


def local(student_hidden, teacher_hidden, student_head, teacher_head, row_weight):
    ds, dt = student_hidden.shape[1], teacher_hidden.shape[1]
    mine = jnp.concatenate([student_hidden, teacher_hidden], axis=1)
    far = lax.all_gather(mine, FAR)
    every = lax.all_to_all(spread(far, student_head, teacher_head), NEAR, 0, 0).reshape(Y * Z * 2, ds + dt)
    student_exp, teacher_exp, tops, log_sums = logits(every, student_head, teacher_head)
    log_sums_of = to_all(log_sums, ALL, Y * Z)
    parts = partial(student_exp, teacher_exp, tops, log_sums_of, student_head)
    near_sums = lax.all_to_all(parts.reshape(Y * L, H * 2, ds), NEAR, 0, 0)
    far_sums = lax.all_to_all(fold(near_sums), FAR, 0, 0)
    summed = jnp.sum(far_sums.astype(jnp.float32), axis=0)
    return (row_weight[:, None] * summed).astype(jnp.bfloat16)


def solution(mesh):
    split = Mesh(mesh.devices.reshape(-1, Y, H, L), ("grp", "y", "h", "l"))
    rows = P(("grp", *ALL))
    head = P(ALL)
    return jax.shard_map(
        local, mesh=split, in_specs=(rows, rows, head, head, rows), out_specs=rows, check_vma=False
    )
```

```python
import jax
import jax.numpy as jnp
from jax import lax
from jax.experimental import pallas as pl
from jax.experimental.pallas import tpu as pltpu
from jax.sharding import Mesh, PartitionSpec as P

Y, Z, L = 4, 16, 2
H = Z // L
NEAR, FAR, ALL = ("y", "l"), ("b", "a"), ("y", "a", "b", "l")
DIMS = (((1,), (1,)), ((), ()))
MIB = 1 << 20
WIDE, DEEP = 2560, 256
IN_VMEM = pl.BlockSpec(memory_space=pltpu.VMEM)
IN_HBM = pl.BlockSpec(memory_space=pltpu.HBM)


def to_all(x, axis, size):
    return lax.all_to_all(jnp.broadcast_to(x[None], (size, *x.shape)), axis, 0, 0)


def far_off(x):
    return pltpu.with_memory_space_constraint(x, pltpu.HBM)


def near(x):
    return pltpu.with_memory_space_constraint(x, pltpu.VMEM)


def spread_kernel(far_ref, student_head, teacher_head, out_ref):
    far = far_ref[...].astype(jnp.float32)
    block = jnp.concatenate([far[i] for i in range(far.shape[0])], axis=0).astype(out_ref.dtype)
    for i in range(out_ref.shape[0]):
        out_ref[i] = block


def spread(far, student_head, teacher_head):
    count, rows, width = far.shape
    return pl.pallas_call(
        spread_kernel,
        out_shape=jax.ShapeDtypeStruct((Y * L, count * rows, width), far.dtype),
        in_specs=[IN_VMEM, IN_HBM, IN_HBM],
        out_specs=IN_VMEM,
        compiler_params=pltpu.CompilerParams(vmem_limit_bytes=8 * MIB),
    )(far, far_off(student_head), far_off(teacher_head))


def fold_kernel(sums_ref, out_ref):
    total = jnp.sum(sums_ref[...].astype(jnp.float32), axis=0)
    for i in range(out_ref.shape[0]):
        out_ref[i] = total[2 * i : 2 * i + 2].astype(out_ref.dtype)


def fold(sums):
    width = sums.shape[2]
    return pl.pallas_call(
        fold_kernel,
        out_shape=jax.ShapeDtypeStruct((H, 2, width), sums.dtype),
        in_specs=[IN_VMEM],
        out_specs=IN_VMEM,
        compiler_params=pltpu.CompilerParams(vmem_limit_bytes=8 * MIB),
    )(sums)


def logits_kernel(rows_ref, student_ref, teacher_ref, student_exp, teacher_exp, tops_ref, sums_ref, scratch):
    rows = rows_ref.shape[0]
    first = 0
    for k, (head, out) in enumerate(((student_ref, student_exp), (teacher_ref, teacher_exp))):
        entries, width = head.shape
        top = None
        for i in range(entries // DEEP):
            part = slice(i * DEEP, (i + 1) * DEEP)
            piece = lax.dot_general(
                head[part, :], rows_ref[:, first : first + width], DIMS, preferred_element_type=jnp.float32
            )
            scratch[part, :] = piece
            most = jnp.max(piece, axis=0, keepdims=True)
            top = most if top is None else jnp.maximum(top, most)
        total = jnp.zeros_like(top)
        for i in range(entries // rows):
            part = slice(i * rows, (i + 1) * rows)
            exp = jnp.exp(scratch[part, :] - top)
            total += jnp.sum(exp, axis=0, keepdims=True)
            out[:, part] = jnp.transpose(exp)
        tops_ref[k : k + 1] = top
        sums_ref[k : k + 1] = top + jnp.log(total)
        first += width


def logits(every, student_head, teacher_head):
    rows, entries = every.shape[0], student_head.shape[0]
    return pl.pallas_call(
        logits_kernel,
        out_shape=(
            jax.ShapeDtypeStruct((rows, entries), jnp.float32),
            jax.ShapeDtypeStruct((rows, entries), jnp.float32),
            jax.ShapeDtypeStruct((2, rows), jnp.float32),
            jax.ShapeDtypeStruct((2, rows), jnp.float32),
        ),
        in_specs=[IN_VMEM] * 3,
        out_specs=[IN_VMEM] * 4,
        scratch_shapes=[pltpu.VMEM((entries, rows), jnp.float32)],
        compiler_params=pltpu.CompilerParams(vmem_limit_bytes=12 * MIB),
    )(every, near(student_head), near(teacher_head))


def partial_kernel(student_exp, teacher_exp, tops_ref, all_ref, head, out, difference):
    rows = student_exp.shape[0]
    most = jnp.max(all_ref[...], axis=0)
    total = jnp.sum(jnp.exp(all_ref[...] - most), axis=0)
    factors = jnp.exp(tops_ref[...] - most) / total
    student_factor = jnp.transpose(jnp.broadcast_to(factors[0:1], (rows, rows)))
    teacher_factor = jnp.transpose(jnp.broadcast_to(factors[1:2], (rows, rows)))
    for i in range(student_exp.shape[1] // rows):
        part = slice(i * rows, (i + 1) * rows)
        difference[:, part] = (
            student_exp[:, part] * student_factor - teacher_exp[:, part] * teacher_factor
        ).astype(difference.dtype)

    for i in range(out.shape[1] // WIDE):
        part = slice(i * WIDE, (i + 1) * WIDE)
        out[:, part] = jnp.dot(
            difference[...], head[:, part], preferred_element_type=jnp.float32
        ).astype(out.dtype)


def partial(student_exp, teacher_exp, tops, sums_of, head):
    rows, entries = student_exp.shape
    return pl.pallas_call(
        partial_kernel,
        out_shape=jax.ShapeDtypeStruct((rows, head.shape[1]), jnp.bfloat16),
        in_specs=[IN_VMEM] * 5,
        out_specs=IN_VMEM,
        scratch_shapes=[pltpu.VMEM((rows, entries), jnp.bfloat16)],
        compiler_params=pltpu.CompilerParams(vmem_limit_bytes=12 * MIB),
    )(student_exp, teacher_exp, tops, sums_of, near(head))


def local(student_hidden, teacher_hidden, student_head, teacher_head, row_weight):
    ds, dt = student_hidden.shape[1], teacher_hidden.shape[1]
    mine = jnp.concatenate([student_hidden, teacher_hidden], axis=1)
    far = lax.all_gather(lax.all_gather(mine, "a"), "b").reshape(H, 2, ds + dt)
    every = lax.all_to_all(spread(far, student_head, teacher_head), NEAR, 0, 0).reshape(Y * Z * 2, ds + dt)
    student_exp, teacher_exp, tops, log_sums = logits(every, student_head, teacher_head)
    log_sums_of = to_all(log_sums, ALL, Y * Z)
    parts = partial(student_exp, teacher_exp, tops, log_sums_of, student_head)
    near_sums = lax.all_to_all(parts.reshape(Y * L, H * 2, ds), NEAR, 0, 0)
    far_sums = lax.all_to_all(fold(near_sums), FAR, 0, 0)
    summed = jnp.sum(far_sums.astype(jnp.float32), axis=0)
    return (row_weight[:, None] * summed).astype(jnp.bfloat16)


def solution(mesh):
    split = Mesh(mesh.devices.reshape(-1, Y, 4, 2, L), ("grp", "y", "a", "b", "l"))
    rows = P(("grp", *ALL))
    head = P(ALL)
    return jax.shard_map(
        local, mesh=split, in_specs=(rows, rows, head, head, rows), out_specs=rows, check_vma=False
    )
```
